32 devices in a mesh: district: 2 (over x), tile: 16 (over z, y, core).
Axes of the slice: x: 2, y: 2, z: 4, core: 2. Of those that a mesh axis runs over, the one named last changes fastest.
Arguments:
- cotangent: bfloat16 [384, 49152], P('tile', 'district'), parts along dimension 1, may hold values from -6 to 6
- coeffs: bfloat16 [2305, 49152], P(None, ('district', 'tile')), parts along dimension 1, may hold values from -0.0390625 to 0.0390625
- ctf: float32 [8, 24], replicated, may hold values from -1.5 to 1.5
- tap_count: int32 [8], replicated, may hold values from 1 to 24, as said below
- construction: int32 [49152], P('district'), parts along dimension 0, may hold values from 0 to 7
Outputs:
- sky_grad: float32 [384, 4610], P('tile', 'district'), parts along dimension 1
The draws below stay inside these ranges and needn't reach their ends.
There are 2 independent parts, one for each index of `district`. The reference program is written for one: setup_inputs(seed, part) draws one part's arguments, and reference() takes and returns one part's arrays. A program takes and returns all parts, laid end to end along the dimension named above; an argument that names none is the same for every part. Nothing has to cross between parts.
Inputs may be any that keep to these rules, and one draw needn't show every extreme that they name: `tap_count`: some type has 24 live taps and some has one.
All inputs are finite; a program needn't handle non-finite values.
Results may differ from the reference program's by a relative error of at most 0.0029.
Values may be sent and summed in bfloat16 or wider, within the bound.
A program may use at most 128 MiB of HBM per device.

```python
import jax
import jax.numpy as jnp
from jax import lax

PATCHES = 2305
TAPS = 24
NTYPES = 8
S_DEV = 1536
TIME = 384
POINTS = 24576
N_TILE = 16


def draw_tap_count(key, part):
    counts = jax.random.randint(key, (NTYPES,), 1, TAPS + 1)
    counts = counts.at[0].set(TAPS)
    counts = counts.at[1].set(1)
    return counts.astype(jnp.int32)


def touch_ends(entries, own_key, least, high):
    extent = entries.shape
    place = [jax.random.randint(jax.random.fold_in(own_key, axis), (), 0, extent[axis]) for axis in range(len(extent))]
    entries = entries.at[tuple(place)].set(least)
    longest = extent.index(max(extent))
    place[longest] = (place[longest] + 1) % extent[longest]
    return entries.at[tuple(place)].set(high)


def block_scale(rng, dims, shards, smallest, high):
    loudness = 1.0
    for position, shards_of in shards:
        draws = jax.random.uniform(jax.random.fold_in(jax.random.fold_in(rng, 6), position), (shards_of,), jnp.float32, smallest / len(shards), high / len(shards))
        loudness = loudness * jnp.repeat(jnp.exp(draws), dims[position] // shards_of).reshape((-1,) + (1,) * (len(dims) - 1 - position))
    return loudness


def gaussian(own_key, shape, scale, limit, split=(), kind=jnp.bfloat16):
    result = scale * jax.random.normal(own_key, shape, jnp.float32)
    if split:
        result = result * block_scale(own_key, shape, split, -0.22, 0.18)
    return jnp.clip(result, -limit, limit).astype(kind)


def setup_inputs(seed: int = 0, part: int = 0) -> dict:
    streams_of = jax.random.split(jax.random.key(seed), 6)
    part_keys = jax.random.split(jax.random.fold_in(streams_of[5], part), 6)
    cotangent = gaussian(part_keys[0], (TIME, POINTS), 1.0, 6.0, ((0, 16),))
    coeffs = gaussian(part_keys[1], (PATCHES, POINTS), POINTS ** -0.5, 0.0390625, ((1, 16),))
    ctf = gaussian(streams_of[2], (NTYPES, TAPS), 0.25, 1.5, (), jnp.float32)
    tap_count = draw_tap_count(jax.random.fold_in(streams_of[5], 71), part)
    construction = touch_ends(jax.random.randint(part_keys[4], (POINTS,), 0, NTYPES), jax.random.fold_in(part_keys[4], 1), 0, NTYPES - 1).astype(jnp.int32)
    return {"cotangent": cotangent, "coeffs": coeffs, "ctf": ctf, "tap_count": tap_count, "construction": construction}


def taps_table(construction, tap_count, ctf):
    onehot = (construction[:, None] == jnp.arange(NTYPES, dtype=jnp.int32)[None, :]).astype(jnp.float32)
    live = jnp.where(jnp.arange(TAPS, dtype=jnp.int32)[None, :] < tap_count[:, None], ctf, jnp.float32(0.0))
    return jnp.einsum("sc,ck->ks", onehot, live.astype(jnp.float32), precision=lax.Precision.HIGHEST)


def reference(cotangent, coeffs, ctf, tap_count, construction):
    def one_block(total, block):
        start = (block * S_DEV).astype(jnp.int32)
        rows = lax.dynamic_slice_in_dim(cotangent, start, S_DEV, 1)
        cols = lax.dynamic_slice_in_dim(coeffs, start, S_DEV, 1)
        kinds = lax.dynamic_slice_in_dim(construction, start, S_DEV, 0)
        taps = taps_table(kinds, tap_count, ctf)
        padded = jnp.concatenate([rows.astype(jnp.float32), jnp.zeros((TAPS - 1, S_DEV), jnp.float32)], 0)
        accum = jnp.zeros((TIME, S_DEV), jnp.float32)
        for shift_k in range(TAPS):
            accum = accum + taps[shift_k][None, :] * padded[shift_k:shift_k + TIME]
        surface = accum.astype(jnp.bfloat16)
        term = lax.dot_general(surface, cols, (((1,), (1,)), ((), ())), preferred_element_type=jnp.float32)
        return total + term, None

    total, unused = lax.scan(one_block, jnp.zeros((TIME, PATCHES), jnp.float32), jnp.arange(N_TILE, dtype=jnp.int32))
    return total
```

```python
import functools

import jax
import jax.numpy as jnp
from jax import lax
from jax.experimental import pallas as pl
from jax.experimental.pallas import tpu as pltpu
from jax.sharding import PartitionSpec as P

MESH = pl.DeviceIdType.MESH
LANES = 128
CHUNK = 256
PLANE = 4


def kernel(
    n, cot, coeffs, kinds_all, ctf, tap_count, out,
    recv, weights, kinds, taps, ext, surf, csend, crecv, keep, ysend, yrecv, ykeep, zsend, zrecv,
    a_send, a_recv, c_send, c_recv, y_send, y_recv, z_send, z_recv, local,
):
    hours = cot.shape[0]
    points = coeffs.shape[1]
    patches = coeffs.shape[0]
    span = ctf.shape[1]
    types = ctf.shape[0]
    groups = n // PLANE
    rows = PLANE * hours
    tiles = points // LANES
    whole = patches // CHUNK
    main = whole * CHUNK

    me = lax.axis_index("tile")
    core = lax.rem(me, 2)
    ypos = lax.rem(me // 2, 2)
    zpos = me // PLANE
    core_peer = me + 1 - 2 * core
    y_peer = me + 2 - 4 * ypos

    load_w = pltpu.make_async_copy(coeffs, weights, local.at[0])
    load_w.start()
    load_k = pltpu.make_async_copy(
        kinds_all.at[:, pl.ds(pl.multiple_of(me * points, LANES), points)], kinds, local.at[1]
    )
    load_k.start()

    def columns(dst):
        return cot.at[:, pl.ds(pl.multiple_of(dst * points, LANES), points)]

    own = pltpu.make_async_copy(columns(me), recv.at[me], local.at[2])
    own.start()

    barrier = pltpu.get_barrier_semaphore()

    def greet(d, carry):
        pl.semaphore_signal(
            barrier, inc=1, device_id={"tile": lax.rem(me + d, n)}, device_id_type=MESH
        )
        return carry

    lax.fori_loop(1, n, greet, 0)
    pl.semaphore_wait(barrier, n - 1)

    def block_copy(src, dst):
        return pltpu.make_async_remote_copy(
            src_ref=columns(dst),
            dst_ref=recv.at[src],
            send_sem=a_send.at[dst],
            recv_sem=a_recv.at[src],
            device_id={"tile": dst},
            device_id_type=MESH,
        )

    offsets = [n // 2]
    for step in range(1, n // 2):
        offsets += [n // 2 - step, n // 2 + step]
    for d in offsets:
        block_copy(me, lax.rem(me + d, n)).start()

    load_k.wait()
    kind = jnp.broadcast_to(kinds[...], (8, points))
    for k in range(span):
        row = jnp.zeros((8, points), jnp.float32)
        for c in range(types):
            live = jnp.where(k < tap_count[c], ctf[c, k], jnp.float32(0.0))
            row = jnp.where(kind == c, live, row)
        taps[k] = row

    for d in range(1, n):
        block_copy(lax.rem(me + d, n), me).wait_recv()
    own.wait()
    load_w.wait()

    def core_copy(i):
        return pltpu.make_async_remote_copy(
            src_ref=csend.at[i], dst_ref=crecv.at[i], send_sem=c_send.at[i],
            recv_sem=c_recv.at[i], device_id={"tile": core_peer}, device_id_type=MESH,
        )

    def y_copy(i):
        return pltpu.make_async_remote_copy(
            src_ref=ysend.at[i], dst_ref=yrecv.at[i], send_sem=y_send.at[i],
            recv_sem=y_recv.at[i], device_id={"tile": y_peer}, device_id_type=MESH,
        )

    def z_copy(src, dst):
        return pltpu.make_async_remote_copy(
            src_ref=zsend.at[dst], dst_ref=zrecv.at[src], send_sem=z_send.at[dst],
            recv_sem=z_recv.at[src], device_id={"tile": dst * PLANE + lax.rem(me, PLANE)},
            device_id_type=MESH,
        )

    def group_at(i):
        return lax.rem(zpos + 1 + i, groups)

    def compute(i):
        g = group_at(i)
        slot = i % 2

        def fir(ct, carry):
            cols = pl.ds(pl.multiple_of(ct * LANES, LANES), LANES)
            for b in range(PLANE):
                ext[pl.ds(b * hours, hours), :] = recv[g * PLANE + b, :, cols].astype(jnp.float32)
            after = recv[lax.rem(g * PLANE + PLANE, n), :, cols].astype(jnp.float32)
            ext[pl.ds(rows, hours), :] = jnp.where(g < groups - 1, after, jnp.zeros_like(after))
            acc = [jnp.zeros((8, LANES), jnp.float32) for _ in range(rows // 8)]
            for k in range(span):
                tap = taps[k, :, cols]
                for r in range(rows // 8):
                    acc[r] = acc[r] + tap * ext[pl.ds(r * 8 + k, 8), :]
            surf[:, cols] = jnp.concatenate(acc, 0).astype(jnp.bfloat16)
            return carry

        lax.fori_loop(0, tiles, fir, 0)

        def emit(value, cols):
            for y in range(2):
                first = value[(2 * y) * hours:(2 * y + 1) * hours]
                second = value[(2 * y + 1) * hours:(2 * y + 2) * hours]
                csend[i, y, :, cols] = jnp.where(core == 0, second, first).astype(jnp.bfloat16)
                keep[slot, y, :, cols] = jnp.where(core == 0, first, second)

        def mm(j, carry):
            at = pl.ds(pl.multiple_of(j * CHUNK, CHUNK), CHUNK)
            emit(
                lax.dot_general(
                    surf[...], weights[at, :], (((1,), (1,)), ((), ())),
                    preferred_element_type=jnp.float32,
                ),
                at,
            )
            return carry

        lax.fori_loop(0, whole, mm, 0)
        rest = patches - main
        if rest:
            last = lax.dot_general(
                surf[...], weights[pl.ds(main, rest), :], (((1,), (1,)), ((), ())),
                preferred_element_type=jnp.float32,
            ) if rest > 1 else jnp.sum(
                surf[...].astype(jnp.float32) * weights[pl.ds(main, 1), :].astype(jnp.float32),
                axis=1, keepdims=True,
            )
            width = keep.shape[-1] - main
            if width != rest:
                last = jnp.where(
                    lax.broadcasted_iota(jnp.int32, (rows, width), 1) < rest,
                    jnp.broadcast_to(last, (rows, width)),
                    jnp.float32(0.0),
                )
            emit(last, pl.ds(main, width))
        core_copy(i).start()

    def core_done(i):
        slot = i % 2
        core_copy(i).wait_recv()
        ysend[i] = (keep[slot, 1 - ypos] + crecv[i, 1 - ypos].astype(jnp.float32)).astype(
            jnp.bfloat16
        )
        y_copy(i).start()
        ykeep[slot] = keep[slot, ypos] + crecv[i, ypos].astype(jnp.float32)

    def y_done(i):
        slot = i % 2
        y_copy(i).wait_recv()
        value = ykeep[slot] + yrecv[i].astype(jnp.float32)
        if i < groups - 1:
            g = group_at(i)
            zsend[g] = value.astype(jnp.bfloat16)
            z_copy(zpos, g).start()
        else:
            ykeep[slot] = value

    for i in range(groups + 2):
        if i < groups:
            compute(i)
        if i >= 2:
            y_done(i - 2)
        if 1 <= i <= groups:
            core_done(i - 1)

    total = ykeep[(groups - 1) % 2]
    for d in range(1, groups):
        src = lax.rem(zpos + d, groups)
        z_copy(src, zpos).wait_recv()
        total = total + zrecv[src].astype(jnp.float32)
    out[...] = total[:, :patches]

    for d in range(1, n):
        block_copy(me, lax.rem(me + d, n)).wait_send()
    for i in range(groups):
        core_copy(i).wait_send()
        y_copy(i).wait_send()
        if i < groups - 1:
            z_copy(zpos, group_at(i)).wait_send()


def per_device(n, cotangent, coeffs, ctf, tap_count, construction):
    hours = cotangent.shape[0]
    patches, points = coeffs.shape
    groups = n // PLANE
    width = -(-patches // LANES) * LANES
    span = ctf.shape[1]
    rows = PLANE * hours
    bf16, f32 = jnp.bfloat16, jnp.float32
    dma = pltpu.SemaphoreType.DMA
    return pl.pallas_call(
        functools.partial(kernel, n),
        out_shape=jax.ShapeDtypeStruct((hours, patches), f32),
        in_specs=[
            pl.BlockSpec(memory_space=pltpu.HBM),
            pl.BlockSpec(memory_space=pltpu.HBM),
            pl.BlockSpec(memory_space=pltpu.HBM),
            pl.BlockSpec(memory_space=pltpu.SMEM),
            pl.BlockSpec(memory_space=pltpu.SMEM),
        ],
        out_specs=pl.BlockSpec(memory_space=pltpu.VMEM),
        scratch_shapes=[
            pltpu.VMEM((n, hours, points), bf16),
            pltpu.VMEM((patches, points), bf16),
            pltpu.VMEM((1, points), jnp.int32),
            pltpu.VMEM((span, 8, points), f32),
            pltpu.VMEM((rows + hours, LANES), f32),
            pltpu.VMEM((rows, points), bf16),
            pltpu.VMEM((groups, 2, hours, width), bf16),
            pltpu.VMEM((groups, 2, hours, width), bf16),
            pltpu.VMEM((2, 2, hours, width), f32),
            pltpu.VMEM((groups, hours, width), bf16),
            pltpu.VMEM((groups, hours, width), bf16),
            pltpu.VMEM((2, hours, width), f32),
            pltpu.VMEM((groups, hours, width), bf16),
            pltpu.VMEM((groups, hours, width), bf16),
            dma((n,)),
            dma((n,)),
            dma((groups,)),
            dma((groups,)),
            dma((groups,)),
            dma((groups,)),
            dma((groups,)),
            dma((groups,)),
            dma((3,)),
        ],
        compiler_params=pltpu.CompilerParams(
            collective_id=0, has_side_effects=True, vmem_limit_bytes=56 * 2**20
        ),
        name="sky_adjoint",
    )(cotangent, coeffs, construction.reshape(1, -1), ctf, tap_count)


def solution(mesh):
    return jax.shard_map(
        functools.partial(per_device, mesh.shape["tile"]),
        mesh=mesh,
        in_specs=(P("tile", "district"), P(None, ("district", "tile")), P(), P(), P("district")),
        out_specs=P("tile", "district"),
        check_vma=False,
    )
```

```python
import functools

import jax
import jax.numpy as jnp
from jax import lax
from jax.experimental import pallas as pl
from jax.experimental.pallas import tpu as pltpu
from jax.sharding import PartitionSpec as P

MESH = pl.DeviceIdType.MESH
LANES = 128
CHUNK = 768
PLANE = 4
UNITS = 3


def kernel(
    n, cot, coeffs, kinds_all, ctf, tap_count, out,
    recv, weights, kinds, taps, ext, surf, csend, crecv, keep, ysend, yrecv, ykeep, zsend, zrecv,
    a_send, a_recv, c_send, c_recv, y_send, y_recv, z_send, z_recv, local,
):
    hours = cot.shape[0]
    points = coeffs.shape[1]
    patches = coeffs.shape[0]
    span = ctf.shape[1]
    types = ctf.shape[0]
    groups = n // PLANE
    rows = PLANE * hours
    tiles = points // LANES
    whole = patches // CHUNK
    main = whole * CHUNK

    me = lax.axis_index("tile")
    core = lax.rem(me, 2)
    ypos = lax.rem(me // 2, 2)
    zpos = me // PLANE
    core_peer = me + 1 - 2 * core
    y_peer = me + 2 - 4 * ypos

    load_w = pltpu.make_async_copy(coeffs, weights, local.at[0])
    load_w.start()
    load_k = pltpu.make_async_copy(
        kinds_all.at[:, pl.ds(pl.multiple_of(me * points, LANES), points)], kinds, local.at[1]
    )
    load_k.start()

    def columns(dst):
        return cot.at[:, pl.ds(pl.multiple_of(dst * points, LANES), points)]

    own = pltpu.make_async_copy(columns(me), recv.at[me], local.at[2])
    own.start()

    barrier = pltpu.get_barrier_semaphore()

    def greet(d, carry):
        pl.semaphore_signal(
            barrier, inc=1, device_id={"tile": lax.rem(me + d, n)}, device_id_type=MESH
        )
        return carry

    lax.fori_loop(1, n, greet, 0)
    pl.semaphore_wait(barrier, n - 1)

    def block_copy(src, dst):
        return pltpu.make_async_remote_copy(
            src_ref=columns(dst),
            dst_ref=recv.at[src],
            send_sem=a_send.at[dst],
            recv_sem=a_recv.at[src],
            device_id={"tile": dst},
            device_id_type=MESH,
        )

    offsets = [n // 2]
    for step in range(1, n // 2):
        offsets += [n // 2 - step, n // 2 + step]
    for d in offsets:
        block_copy(me, lax.rem(me + d, n)).start()

    load_k.wait()
    kind = jnp.broadcast_to(kinds[...], (8, points))
    for k in range(span):
        row = jnp.zeros((8, points), jnp.float32)
        for c in range(types):
            live = jnp.where(k < tap_count[c], ctf[c, k], jnp.float32(0.0))
            row = jnp.where(kind == c, live, row)
        taps[k] = row

    for d in range(1, n):
        block_copy(lax.rem(me + d, n), me).wait_recv()
    own.wait()
    load_w.wait()

    width = keep.shape[-1]
    units = UNITS if whole % UNITS == 0 else 1
    step = main // units
    block = 4 if groups % 4 == 0 else 1

    def span_of(u):
        return pl.ds(u * step, step if u < units - 1 else width - u * step)

    def core_copy(u):
        return pltpu.make_async_remote_copy(
            src_ref=csend.at[:, :, :, span_of(u)], dst_ref=crecv.at[:, :, :, span_of(u)],
            send_sem=c_send.at[u], recv_sem=c_recv.at[u],
            device_id={"tile": core_peer}, device_id_type=MESH,
        )

    def y_copy(u):
        return pltpu.make_async_remote_copy(
            src_ref=ysend.at[:, :, span_of(u)], dst_ref=yrecv.at[:, :, span_of(u)],
            send_sem=y_send.at[u], recv_sem=y_recv.at[u],
            device_id={"tile": y_peer}, device_id_type=MESH,
        )

    def z_copy(src, dst, u):
        return pltpu.make_async_remote_copy(
            src_ref=zsend.at[dst, :, span_of(u)], dst_ref=zrecv.at[src, :, span_of(u)],
            send_sem=z_send.at[dst, u], recv_sem=z_recv.at[src, u],
            device_id={"tile": dst * PLANE + lax.rem(me, PLANE)}, device_id_type=MESH,
        )

    def fir_group(g, carry):
        def fir(ct, carry):
            cols = pl.ds(pl.multiple_of(ct * LANES, LANES), LANES)
            for b in range(PLANE):
                ext[pl.ds(b * hours, hours), :] = recv[g * PLANE + b, :, cols].astype(jnp.float32)
            after = recv[lax.rem(g * PLANE + PLANE, n), :, cols].astype(jnp.float32)
            ext[pl.ds(rows, hours), :] = jnp.where(g < groups - 1, after, jnp.zeros_like(after))
            acc = [jnp.zeros((8, LANES), jnp.float32) for _ in range(rows // 8)]
            for k in range(span):
                tap = taps[k, :, cols]
                for r in range(rows // 8):
                    acc[r] = acc[r] + tap * ext[pl.ds(r * 8 + k, 8), :]
            at = pl.ds(pl.multiple_of(g * rows, rows), rows)
            surf[at, cols] = jnp.concatenate(acc, 0).astype(jnp.bfloat16)
            return carry

        lax.fori_loop(0, tiles, fir, 0)
        return carry

    lax.fori_loop(0, groups, fir_group, 0)

    def emit(value, mb, cols):
        for q in range(block):
            for y in range(2):
                top = (PLANE * q + 2 * y) * hours
                first = value[top:top + hours]
                second = value[top + hours:top + 2 * hours]
                g = mb * block + q
                csend[g, y, :, cols] = jnp.where(core == 0, second, first).astype(jnp.bfloat16)
                keep[g, y, :, cols] = jnp.where(core == 0, first, second)

    def band(mb):
        return surf[pl.ds(pl.multiple_of(mb * block * rows, block * rows), block * rows), :]

    def compute(u):
        def mm(j, carry):
            at = pl.ds(pl.multiple_of(j * CHUNK, CHUNK), CHUNK)

            def part(mb, carry):
                emit(
                    lax.dot_general(
                        band(mb), weights[at, :], (((1,), (1,)), ((), ())),
                        preferred_element_type=jnp.float32,
                    ),
                    mb, at,
                )
                return carry

            return lax.fori_loop(0, groups // block, part, carry)

        lax.fori_loop(u * (whole // units), (u + 1) * (whole // units), mm, 0)
        core_copy(u).start()

    rest = patches - main

    def edge(mb, carry):
        if rest == 1:
            last = jnp.sum(
                band(mb).astype(jnp.float32) * weights[pl.ds(main, 1), :].astype(jnp.float32),
                axis=1, keepdims=True,
            )
        else:
            last = lax.dot_general(
                band(mb), weights[pl.ds(main, rest), :], (((1,), (1,)), ((), ())),
                preferred_element_type=jnp.float32,
            )
        shape = (block * rows, width - main)
        if width - main != rest:
            last = jnp.where(
                lax.broadcasted_iota(jnp.int32, shape, 1) < rest,
                jnp.broadcast_to(last, shape),
                jnp.float32(0.0),
            )
        emit(last, mb, pl.ds(main, width - main))
        return carry

    if rest:
        lax.fori_loop(0, groups // block, edge, 0)

    def core_done(u):
        cols = span_of(u)
        core_copy(u).wait_recv()
        for g in range(groups):
            ysend[g, :, cols] = (
                keep[g, 1 - ypos, :, cols] + crecv[g, 1 - ypos, :, cols].astype(jnp.float32)
            ).astype(jnp.bfloat16)
        y_copy(u).start()
        for g in range(groups):
            ykeep[g, :, cols] = keep[g, ypos, :, cols] + crecv[g, ypos, :, cols].astype(jnp.float32)

    def y_done(u):
        cols = span_of(u)
        y_copy(u).wait_recv()
        for d in range(1, groups):
            g = lax.rem(zpos + d, groups)
            zsend[g, :, cols] = (
                ykeep[g, :, cols] + yrecv[g, :, cols].astype(jnp.float32)
            ).astype(jnp.bfloat16)
            z_copy(zpos, g, u).start()

    for u in range(units + 2):
        if u < units:
            compute(u)
        if 1 <= u <= units:
            core_done(u - 1)
        if u >= 2:
            y_done(u - 2)

    for u in range(units):
        cols = span_of(u)
        total = ykeep[zpos, :, cols] + yrecv[zpos, :, cols].astype(jnp.float32)
        for d in range(1, groups):
            src = lax.rem(zpos + d, groups)
            z_copy(src, zpos, u).wait_recv()
            total = total + zrecv[src, :, cols].astype(jnp.float32)
        size = step if u < units - 1 else patches - u * step
        out[:, pl.ds(u * step, size)] = total[:, :size]

    for d in range(1, n):
        block_copy(me, lax.rem(me + d, n)).wait_send()
    for u in range(units):
        core_copy(u).wait_send()
        y_copy(u).wait_send()
        for d in range(1, groups):
            z_copy(zpos, lax.rem(zpos + d, groups), u).wait_send()


def per_device(n, cotangent, coeffs, ctf, tap_count, construction):
    hours = cotangent.shape[0]
    patches, points = coeffs.shape
    groups = n // PLANE
    width = -(-patches // LANES) * LANES
    span = ctf.shape[1]
    rows = PLANE * hours
    bf16, f32 = jnp.bfloat16, jnp.float32
    dma = pltpu.SemaphoreType.DMA
    return pl.pallas_call(
        functools.partial(kernel, n),
        out_shape=jax.ShapeDtypeStruct((hours, patches), f32),
        in_specs=[
            pl.BlockSpec(memory_space=pltpu.HBM),
            pl.BlockSpec(memory_space=pltpu.HBM),
            pl.BlockSpec(memory_space=pltpu.HBM),
            pl.BlockSpec(memory_space=pltpu.SMEM),
            pl.BlockSpec(memory_space=pltpu.SMEM),
        ],
        out_specs=pl.BlockSpec(memory_space=pltpu.VMEM),
        scratch_shapes=[
            pltpu.VMEM((n, hours, points), bf16),
            pltpu.VMEM((patches, points), bf16),
            pltpu.VMEM((1, points), jnp.int32),
            pltpu.VMEM((span, 8, points), f32),
            pltpu.VMEM((rows + hours, LANES), f32),
            pltpu.VMEM((groups * rows, points), bf16),
            pltpu.VMEM((groups, 2, hours, width), bf16),
            pltpu.VMEM((groups, 2, hours, width), bf16),
            pltpu.VMEM((groups, 2, hours, width), f32),
            pltpu.VMEM((groups, hours, width), bf16),
            pltpu.VMEM((groups, hours, width), bf16),
            pltpu.VMEM((groups, hours, width), f32),
            pltpu.VMEM((groups, hours, width), bf16),
            pltpu.VMEM((groups, hours, width), bf16),
            dma((n,)),
            dma((n,)),
            dma((UNITS,)),
            dma((UNITS,)),
            dma((UNITS,)),
            dma((UNITS,)),
            dma((groups, UNITS)),
            dma((groups, UNITS)),
            dma((3,)),
        ],
        compiler_params=pltpu.CompilerParams(
            collective_id=0, has_side_effects=True, vmem_limit_bytes=56 * 2**20
        ),
        name="sky_adjoint",
    )(cotangent, coeffs, construction.reshape(1, -1), ctf, tap_count)


def solution(mesh):
    return jax.shard_map(
        functools.partial(per_device, mesh.shape["tile"]),
        mesh=mesh,
        in_specs=(P("tile", "district"), P(None, ("district", "tile")), P(), P(), P("district")),
        out_specs=P("tile", "district"),
        check_vma=False,
    )
```

```python
import functools

import jax
import jax.numpy as jnp
from jax import lax
from jax.experimental import pallas as pl
from jax.experimental.pallas import tpu as pltpu
from jax.sharding import PartitionSpec as P

MESH = pl.DeviceIdType.MESH
LANES = 128
CHUNK = 768
PLANE = 4
UNITS = 3


def kernel(
    n, cot, coeffs, kinds_all, ctf, tap_count, out,
    recv, weights, kinds, taps, ext, surf, csend, crecv, keep, ysend, yrecv, ykeep, zsend, zrecv,
    a_send, a_recv, c_send, c_recv, y_send, y_recv, z_send, z_recv, local,
):
    hours = cot.shape[0]
    points = coeffs.shape[1]
    patches = coeffs.shape[0]
    span = ctf.shape[1]
    types = ctf.shape[0]
    groups = n // PLANE
    rows = PLANE * hours
    tiles = points // LANES
    whole = patches // CHUNK
    main = whole * CHUNK

    me = lax.axis_index("tile")
    core = lax.rem(me, 2)
    ypos = lax.rem(me // 2, 2)
    zpos = me // PLANE
    core_peer = me + 1 - 2 * core
    y_peer = me + 2 - 4 * ypos

    load_w = pltpu.make_async_copy(coeffs, weights, local.at[0])
    load_w.start()
    load_k = pltpu.make_async_copy(
        kinds_all.at[:, pl.ds(pl.multiple_of(me * points, LANES), points)], kinds, local.at[1]
    )
    load_k.start()

    def columns(dst):
        return cot.at[:, pl.ds(pl.multiple_of(dst * points, LANES), points)]

    own = pltpu.make_async_copy(columns(me), recv.at[me], local.at[2])
    own.start()

    barrier = pltpu.get_barrier_semaphore()

    def greet(d, carry):
        pl.semaphore_signal(
            barrier, inc=1, device_id={"tile": lax.rem(me + d, n)}, device_id_type=MESH
        )
        return carry

    lax.fori_loop(1, n, greet, 0)
    pl.semaphore_wait(barrier, n - 1)

    def block_copy(src, dst):
        return pltpu.make_async_remote_copy(
            src_ref=columns(dst),
            dst_ref=recv.at[src],
            send_sem=a_send.at[dst],
            recv_sem=a_recv.at[src],
            device_id={"tile": dst},
            device_id_type=MESH,
        )

    offsets = [n // 2]
    for step in range(1, n // 2):
        offsets += [n // 2 - step, n // 2 + step]
    for d in offsets:
        block_copy(me, lax.rem(me + d, n)).start()

    load_k.wait()
    kind = jnp.broadcast_to(kinds[...], (8, points))
    for k in range(span):
        row = jnp.zeros((8, points), jnp.float32)
        for c in range(types):
            live = jnp.where(k < tap_count[c], ctf[c, k], jnp.float32(0.0))
            row = jnp.where(kind == c, live, row)
        taps[k] = row

    own.wait()
    low = zpos < groups // 2

    def arrive(b):
        @pl.when(me != b)
        def _():
            block_copy(b, me).wait_recv()

    def arrive_group(i):
        @pl.when(low)
        def _():
            if i == 0:
                arrive(0)
            for b in range(PLANE * i + 1, min(PLANE * (i + 1) + 1, n)):
                arrive(b)

        @pl.when(jnp.logical_not(low))
        def _():
            for b in range(PLANE * (groups - 1 - i), PLANE * (groups - i)):
                arrive(b)


    width = keep.shape[-1]
    units = UNITS if whole % UNITS == 0 else 1
    step = main // units
    block = 4 if groups % 4 == 0 else 1

    def span_of(u):
        return pl.ds(u * step, step if u < units - 1 else width - u * step)

    def core_copy(u):
        return pltpu.make_async_remote_copy(
            src_ref=csend.at[:, :, :, span_of(u)], dst_ref=crecv.at[:, :, :, span_of(u)],
            send_sem=c_send.at[u], recv_sem=c_recv.at[u],
            device_id={"tile": core_peer}, device_id_type=MESH,
        )

    def y_copy(u):
        return pltpu.make_async_remote_copy(
            src_ref=ysend.at[:, :, span_of(u)], dst_ref=yrecv.at[:, :, span_of(u)],
            send_sem=y_send.at[u], recv_sem=y_recv.at[u],
            device_id={"tile": y_peer}, device_id_type=MESH,
        )

    def z_copy(src, dst, u):
        return pltpu.make_async_remote_copy(
            src_ref=zsend.at[dst, :, span_of(u)], dst_ref=zrecv.at[src, :, span_of(u)],
            send_sem=z_send.at[dst, u], recv_sem=z_recv.at[src, u],
            device_id={"tile": dst * PLANE + lax.rem(me, PLANE)}, device_id_type=MESH,
        )

    def fir_group(g, carry):
        def fir(ct, carry):
            cols = pl.ds(pl.multiple_of(ct * LANES, LANES), LANES)
            for b in range(PLANE):
                ext[pl.ds(b * hours, hours), :] = recv[g * PLANE + b, :, cols].astype(jnp.float32)
            after = recv[jnp.minimum(g * PLANE + PLANE, n - 1), :, cols].astype(jnp.float32)
            ext[pl.ds(rows, hours), :] = jnp.where(g < groups - 1, after, jnp.zeros_like(after))
            acc = [jnp.zeros((8, LANES), jnp.float32) for _ in range(rows // 8)]
            for k in range(span):
                tap = taps[k, :, cols]
                for r in range(rows // 8):
                    acc[r] = acc[r] + tap * ext[pl.ds(r * 8 + k, 8), :]
            at = pl.ds(pl.multiple_of(g * rows, rows), rows)
            surf[at, cols] = jnp.concatenate(acc, 0).astype(jnp.bfloat16)
            return carry

        lax.fori_loop(0, tiles, fir, 0)
        return carry

    for i in range(groups):
        arrive_group(i)
        fir_group(jnp.where(low, i, groups - 1 - i), 0)
    load_w.wait()

    def emit(value, mb, cols):
        for q in range(block):
            for y in range(2):
                top = (PLANE * q + 2 * y) * hours
                first = value[top:top + hours]
                second = value[top + hours:top + 2 * hours]
                g = mb * block + q
                csend[g, y, :, cols] = jnp.where(core == 0, second, first).astype(jnp.bfloat16)
                keep[g, y, :, cols] = jnp.where(core == 0, first, second)

    def band(mb):
        return surf[pl.ds(pl.multiple_of(mb * block * rows, block * rows), block * rows), :]

    def compute(u):
        def mm(j, carry):
            at = pl.ds(pl.multiple_of(j * CHUNK, CHUNK), CHUNK)

            def part(mb, carry):
                emit(
                    lax.dot_general(
                        band(mb), weights[at, :], (((1,), (1,)), ((), ())),
                        preferred_element_type=jnp.float32,
                    ),
                    mb, at,
                )
                return carry

            return lax.fori_loop(0, groups // block, part, carry)

        lax.fori_loop(u * (whole // units), (u + 1) * (whole // units), mm, 0)
        core_copy(u).start()

    rest = patches - main

    def edge(mb, carry):
        if rest == 1:
            last = jnp.sum(
                band(mb).astype(jnp.float32) * weights[pl.ds(main, 1), :].astype(jnp.float32),
                axis=1, keepdims=True,
            )
        else:
            last = lax.dot_general(
                band(mb), weights[pl.ds(main, rest), :], (((1,), (1,)), ((), ())),
                preferred_element_type=jnp.float32,
            )
        shape = (block * rows, width - main)
        if width - main != rest:
            last = jnp.where(
                lax.broadcasted_iota(jnp.int32, shape, 1) < rest,
                jnp.broadcast_to(last, shape),
                jnp.float32(0.0),
            )
        emit(last, mb, pl.ds(main, width - main))
        return carry

    if rest:
        lax.fori_loop(0, groups // block, edge, 0)

    def core_done(u):
        cols = span_of(u)
        core_copy(u).wait_recv()
        for g in range(groups):
            ysend[g, :, cols] = (
                keep[g, 1 - ypos, :, cols] + crecv[g, 1 - ypos, :, cols].astype(jnp.float32)
            ).astype(jnp.bfloat16)
        y_copy(u).start()
        for g in range(groups):
            ykeep[g, :, cols] = keep[g, ypos, :, cols] + crecv[g, ypos, :, cols].astype(jnp.float32)

    def y_done(u):
        cols = span_of(u)
        y_copy(u).wait_recv()
        for d in range(1, groups):
            g = lax.rem(zpos + d, groups)
            zsend[g, :, cols] = (
                ykeep[g, :, cols] + yrecv[g, :, cols].astype(jnp.float32)
            ).astype(jnp.bfloat16)
            z_copy(zpos, g, u).start()

    for u in range(units + 2):
        if u < units:
            compute(u)
        if 1 <= u <= units:
            core_done(u - 1)
        if u >= 2:
            y_done(u - 2)

    for u in range(units):
        cols = span_of(u)
        total = ykeep[zpos, :, cols] + yrecv[zpos, :, cols].astype(jnp.float32)
        for d in range(1, groups):
            src = lax.rem(zpos + d, groups)
            z_copy(src, zpos, u).wait_recv()
            total = total + zrecv[src, :, cols].astype(jnp.float32)
        size = step if u < units - 1 else patches - u * step
        out[:, pl.ds(u * step, size)] = total[:, :size]

    for d in range(1, n):
        block_copy(me, lax.rem(me + d, n)).wait_send()
    for u in range(units):
        core_copy(u).wait_send()
        y_copy(u).wait_send()
        for d in range(1, groups):
            z_copy(zpos, lax.rem(zpos + d, groups), u).wait_send()


def per_device(n, cotangent, coeffs, ctf, tap_count, construction):
    hours = cotangent.shape[0]
    patches, points = coeffs.shape
    groups = n // PLANE
    width = -(-patches // LANES) * LANES
    span = ctf.shape[1]
    rows = PLANE * hours
    bf16, f32 = jnp.bfloat16, jnp.float32
    dma = pltpu.SemaphoreType.DMA
    return pl.pallas_call(
        functools.partial(kernel, n),
        out_shape=jax.ShapeDtypeStruct((hours, patches), f32),
        in_specs=[
            pl.BlockSpec(memory_space=pltpu.HBM),
            pl.BlockSpec(memory_space=pltpu.HBM),
            pl.BlockSpec(memory_space=pltpu.HBM),
            pl.BlockSpec(memory_space=pltpu.SMEM),
            pl.BlockSpec(memory_space=pltpu.SMEM),
        ],
        out_specs=pl.BlockSpec(memory_space=pltpu.VMEM),
        scratch_shapes=[
            pltpu.VMEM((n, hours, points), bf16),
            pltpu.VMEM((patches, points), bf16),
            pltpu.VMEM((1, points), jnp.int32),
            pltpu.VMEM((span, 8, points), f32),
            pltpu.VMEM((rows + hours, LANES), f32),
            pltpu.VMEM((groups * rows, points), bf16),
            pltpu.VMEM((groups, 2, hours, width), bf16),
            pltpu.VMEM((groups, 2, hours, width), bf16),
            pltpu.VMEM((groups, 2, hours, width), f32),
            pltpu.VMEM((groups, hours, width), bf16),
            pltpu.VMEM((groups, hours, width), bf16),
            pltpu.VMEM((groups, hours, width), f32),
            pltpu.VMEM((groups, hours, width), bf16),
            pltpu.VMEM((groups, hours, width), bf16),
            dma((n,)),
            dma((n,)),
            dma((UNITS,)),
            dma((UNITS,)),
            dma((UNITS,)),
            dma((UNITS,)),
            dma((groups, UNITS)),
            dma((groups, UNITS)),
            dma((3,)),
        ],
        compiler_params=pltpu.CompilerParams(
            collective_id=0, has_side_effects=True, vmem_limit_bytes=56 * 2**20
        ),
        name="sky_adjoint",
    )(cotangent, coeffs, construction.reshape(1, -1), ctf, tap_count)


def solution(mesh):
    return jax.shard_map(
        functools.partial(per_device, mesh.shape["tile"]),
        mesh=mesh,
        in_specs=(P("tile", "district"), P(None, ("district", "tile")), P(), P(), P("district")),
        out_specs=P("tile", "district"),
        check_vma=False,
    )
```
